32 devices in a mesh: grp: 4 (over z), sub: 8 (over y, x, core).
Axes of the slice: x: 2, y: 2, z: 4, core: 2. Of those that a mesh axis runs over, the one named last changes fastest.
Arguments:
- columns: bfloat16 [8, 65536, 512], P('grp', 'sub'), may hold values from -6 to 6
- in_basis: bfloat16 [8, 65536, 128], P('grp', 'sub'), may hold values from -0.375 to 0.375
- out_basis: bfloat16 [8, 65536, 128], P('grp', 'sub'), may hold values from -0.5 to 0.5
- transfer: bfloat16 [8, 8, 256, 2, 128, 128], P('grp', None, 'sub'), may hold values from -0.375 to 0.375
- true_ranks: int32 [8, 9, 256], P('grp', None, 'sub'), may hold values from 96 to 128
- target: bfloat16 [65536, 512], P('sub'), may hold values from -9 to 9
Outputs:
- gradient: bfloat16 [8, 65536, 512], P('grp', 'sub')
- residual: bfloat16 [65536, 512], P('sub')
The draws below stay inside these ranges and needn't reach their ends.
Inputs may be any that keep to these rules, and one draw needn't show every extreme that they name: true_ranks[g, l, j] is the number of leading rows of block [g, j] that carry data after level l; the remaining rows of the 128 are padding.
All inputs are finite; a program needn't handle non-finite values.
Results may differ from the reference program's by a relative error of at most 0.025.
Values may be sent and summed in bfloat16 or wider, within the bound.
A program may use at most 192 MiB of HBM per device.

```python
import jax
import jax.numpy as jnp
from jax import lax

M = 65536
R = 128
LEVELS = 8
NR = 512
LEAVES = 256
LEAF = 256
BUTTERFLIES = 8


def touch_ends(array, stream_key, least, largest):
    extent = array.shape
    index_at = [jax.random.randint(jax.random.fold_in(stream_key, axis), (), 0, extent[axis]) for axis in range(len(extent))]
    array = array.at[tuple(index_at)].set(least)
    longest = extent.index(max(extent))
    index_at[longest] = (index_at[longest] + 1) % extent[longest]
    return array.at[tuple(index_at)].set(largest)


def level_of(stream_key, shape, shards, least, high):
    loudness = 1.0
    for position, shards_of in shards:
        draws = jax.random.uniform(jax.random.fold_in(jax.random.fold_in(stream_key, 6), position), (shards_of,), jnp.float32, least / len(shards), high / len(shards))
        loudness = loudness * jnp.repeat(jnp.exp(draws), shape[position] // shards_of).reshape((-1,) + (1,) * (len(shape) - 1 - position))
    return loudness


def gaussian(key, shape, spread, reach, split=(), held_as=jnp.bfloat16):
    drawn = spread * jax.random.normal(key, shape, jnp.float32)
    if split:
        drawn = drawn * level_of(key, shape, split, -0.22, 0.18)
    return jnp.clip(drawn, -reach, reach).astype(held_as)


def setup_inputs(seed: int = 0) -> dict:
    arg_keys = jax.random.split(jax.random.key(seed), 7)
    return {
        "columns": gaussian(arg_keys[0], (BUTTERFLIES, M, NR), 1.0, 6.0, ((0, 4), (1, 8))),
        "in_basis": gaussian(arg_keys[1], (BUTTERFLIES, M, R), LEAF ** -0.5, 0.375, ((0, 4), (1, 8))),
        "out_basis": gaussian(arg_keys[2], (BUTTERFLIES, M, R), R ** -0.5, 0.5, ((0, 4), (1, 8))),
        "transfer": gaussian(arg_keys[3], (BUTTERFLIES, LEVELS, LEAVES, 2, R, R), (2 * R) ** -0.5, 0.375, ((0, 4), (2, 8))),
        "true_ranks": touch_ends(jax.random.randint(arg_keys[4], (BUTTERFLIES, LEVELS + 1, LEAVES), R - R // 4, R + 1), jax.random.fold_in(arg_keys[4], 1), R - R // 4, R).astype(jnp.int32),
        "target": gaussian(arg_keys[5], (M, NR), 1.5, 9.0, ((0, 8),)),
    }


def keep_rank(values, rank_row):
    lane_ids = jnp.arange(values.shape[1], dtype=jnp.int32)[None, :, None]
    return jnp.where(lane_ids < rank_row[:, None, None], values, 0.0).astype(jnp.bfloat16)


def flipped(values, stride):
    leaf_count = values.shape[0]
    shaped = values.reshape(leaf_count // (2 * stride), 2, stride, values.shape[1], values.shape[2])
    return jnp.flip(shaped, axis=1).reshape(values.shape)


def forward_one(columns, in_basis, out_basis, transfer, true_ranks):
    column_leaves = columns.reshape(LEAVES, LEAF, NR).astype(jnp.float32)
    in_leaves = in_basis.reshape(LEAVES, LEAF, R).astype(jnp.float32)
    carried = keep_rank(jnp.einsum('jbr,jbn->jrn', in_leaves, column_leaves), true_ranks[0])
    for step_index in range(LEVELS):
        stride = 2 ** step_index
        weights_now = transfer[step_index].astype(jnp.float32)
        source = carried.astype(jnp.float32)
        combined = jnp.einsum('jrq,jqn->jrn', weights_now[:, 0], source)
        combined = combined + jnp.einsum('jrq,jqn->jrn', weights_now[:, 1], flipped(source, stride))
        carried = keep_rank(combined, true_ranks[step_index + 1])
    out_leaves = out_basis.reshape(LEAVES, LEAF, R).astype(jnp.float32)
    return jnp.einsum('jbr,jrn->jbn', out_leaves, carried.astype(jnp.float32)).reshape(M, NR)


def adjoint_one(residual, in_basis, out_basis, transfer, true_ranks):
    out_leaves = out_basis.reshape(LEAVES, LEAF, R).astype(jnp.float32)
    residual_leaves = residual.reshape(LEAVES, LEAF, NR).astype(jnp.float32)
    cotangent = keep_rank(jnp.einsum('jbr,jbn->jrn', out_leaves, residual_leaves), true_ranks[LEVELS])
    for step_index in reversed(range(LEVELS)):
        stride = 2 ** step_index
        weights_now = transfer[step_index].astype(jnp.float32)
        source = cotangent.astype(jnp.float32)
        direct = jnp.einsum('jqr,jqn->jrn', weights_now[:, 0], source)
        across = jnp.einsum('jqr,jqn->jrn', weights_now[:, 1], source).astype(jnp.bfloat16)
        across = lax.optimization_barrier(across)
        cotangent = keep_rank(direct + flipped(across.astype(jnp.float32), stride), true_ranks[step_index])
    in_leaves = in_basis.reshape(LEAVES, LEAF, R).astype(jnp.float32)
    result = jnp.einsum('jbr,jrn->jbn', in_leaves, cotangent.astype(jnp.float32))
    return result.astype(jnp.bfloat16).reshape(M, NR)


def reference(columns, in_basis, out_basis, transfer, true_ranks, target):
    def accumulate(running, pieces):
        image = forward_one(pieces[0], pieces[1], pieces[2], pieces[3], pieces[4])
        return running + image, None

    summed = lax.scan(accumulate, jnp.zeros((M, NR), jnp.float32), (columns, in_basis, out_basis, transfer, true_ranks))[0]
    residual = (summed - target.astype(jnp.float32)).astype(jnp.bfloat16)

    def adjoint_piece(pieces):
        return adjoint_one(residual, pieces[0], pieces[1], pieces[2], pieces[3])

    gradient = lax.map(adjoint_piece, (in_basis, out_basis, transfer, true_ranks))
    return gradient, residual
```

```python
import functools

import jax
import jax.numpy as jnp
from jax import lax
from jax.experimental import pallas as pl
from jax.experimental.pallas import tpu as pltpu
from jax.sharding import PartitionSpec as P

F32 = jnp.float32
BF16 = jnp.bfloat16
VMEM_LIMIT = 54 * 1024 * 1024
COLUMN_PARTS = 2
BLOCK_PARTS = 4


def partner_of(shard, bit):
    return lax.ppermute(shard, "sub", [(i, i ^ 1 << bit) for i in range(lax.axis_size("sub"))])


def dot(a, b):
    return jnp.dot(a, b, preferred_element_type=F32)


def dot_t(a, b):
    return lax.dot_general(a, b, (((0,), (0,)), ((), ())), preferred_element_type=F32)


def keep(values, rank):
    rows = lax.broadcasted_iota(jnp.int32, values.shape, 0)
    return jnp.where(rows < rank, values, 0.0).astype(BF16)


def pair_of(pair, stride):
    low = (pair // stride) * (2 * stride) + pair % stride
    return low, low + stride


def pair_weights(w_ref, level, j, p):
    top = jnp.concatenate([w_ref[0, level, j, 0], w_ref[0, level, j, 1]], axis=1)
    low = jnp.concatenate([w_ref[0, level, p, 1], w_ref[0, level, p, 0]], axis=1)
    return jnp.concatenate([top, low], axis=0)


def start_kernel(local_levels, leaf, ranks, in_ref, col_ref, w_ref, *rest):
    outs, state = rest[:-1], rest[-1]
    g = pl.program_id(0)
    blocks, rank = state.shape[0], state.shape[1]

    def first(j, _):
        rows = pl.ds(pl.multiple_of(j * leaf, leaf), leaf)
        state[j] = keep(dot_t(in_ref[0, rows], col_ref[0, rows]), ranks[g, 0, j])
        return 0

    lax.fori_loop(0, blocks, first, 0, unroll=min(4, blocks))
    for level in range(local_levels):
        def step(pair, _):
            j, p = pair_of(pair, 1 << level)
            both = jnp.concatenate([state[j], state[p]], axis=0)
            made = dot(pair_weights(w_ref, level, j, p), both)
            state[j] = keep(made[:rank], ranks[g, level + 1, j])
            state[p] = keep(made[rank:], ranks[g, level + 1, p])
            return 0

        lax.fori_loop(0, blocks // 2, step, 0, unroll=min(4, blocks // 2))
    part = blocks // len(outs)
    for b, out in enumerate(outs):
        out[0] = state[b * part:(b + 1) * part]


def level_kernel(level, first_block, ranks, s_ref, p_ref, w_ref, out_ref):
    groups, size = s_ref.shape[:2]
    base = first_block + pl.program_id(0) * size
    for g in range(groups):
        for j in range(size):
            both = jnp.concatenate([s_ref[g, j], p_ref[g, j]], axis=0)
            weights = jnp.concatenate([w_ref[g, 0, j, 0], w_ref[g, 0, j, 1]], axis=1)
            out_ref[g, j] = keep(dot(weights, both), ranks[g, level + 1, base + j])


def image_kernel(level, first_block, leaf, ranks, s_ref, p_ref, w_ref, ob_ref, out_ref):
    groups, size = s_ref.shape[:2]
    base = first_block + pl.program_id(0) * size
    for j in range(size):
        rows = slice(j * leaf, (j + 1) * leaf)
        states = []
        for g in range(groups):
            both = jnp.concatenate([s_ref[g, j], p_ref[g, j]], axis=0)
            weights = jnp.concatenate([w_ref[g, 0, j, 0], w_ref[g, 0, j, 1]], axis=1)
            states.append(keep(dot(weights, both), ranks[g, level + 1, base + j]))
        basis = jnp.concatenate([ob_ref[g, rows] for g in range(groups)], axis=1)
        out_ref[rows] = dot(basis, jnp.concatenate(states, axis=0)).astype(BF16)


def residual_kernel(level, first_block, leaf, ranks, sum_ref, target_ref, ob_ref, w_ref, *rest):
    res_ref, back_ref, across_ref = rest[-3:]
    groups, size = back_ref.shape[:2]
    base = first_block + pl.program_id(0) * size
    for j in range(size):
        rows = slice(j * leaf, (j + 1) * leaf)
        residual = (sum_ref[rows].astype(F32) - target_ref[rows].astype(F32)).astype(BF16)
        res_ref[rows] = residual
        for g in range(groups):
            back = keep(dot_t(ob_ref[g, rows], residual), ranks[g, level + 1, base + j])
            back_ref[g, j] = back
            across_ref[g, j] = dot_t(w_ref[g, 0, j, 1], back).astype(BF16)


def back_kernel(level, first_block, ranks, back_ref, arr_ref, w_ref, v_ref, out_ref, across_ref):
    groups, size = back_ref.shape[:2]
    base = first_block + pl.program_id(0) * size
    for g in range(groups):
        for j in range(size):
            made = dot_t(w_ref[g, 0, j, 0], back_ref[g, j]) + arr_ref[g, j].astype(F32)
            back = keep(made, ranks[g, level, base + j])
            out_ref[g, j] = back
            across_ref[g, j] = dot_t(v_ref[g, 0, j, 1], back).astype(BF16)


def end_kernel(local_levels, parts, leaf, ranks, *refs):
    backs, arrs = refs[:parts], refs[parts:2 * parts]
    w_ref, in_ref = refs[2 * parts:2 * parts + 2]
    grad_ref, state = refs[-2:]
    g = pl.program_id(0)
    blocks, rank = state.shape[0], state.shape[1]
    part = blocks // parts
    for b in range(parts):
        def enter(k, _):
            j = b * part + k
            made = dot_t(w_ref[0, local_levels, j, 0], backs[b][0, k]) + arrs[b][0, k].astype(F32)
            state[j] = keep(made, ranks[g, local_levels, j])
            return 0

        lax.fori_loop(0, part, enter, 0, unroll=min(4, part))
    for level in reversed(range(local_levels)):
        def step(pair, _):
            j, p = pair_of(pair, 1 << level)
            both = jnp.concatenate([state[j], state[p]], axis=0)
            made = dot_t(pair_weights(w_ref, level, j, p), both)
            state[j] = keep(made[:rank], ranks[g, level, j])
            state[p] = keep(made[rank:], ranks[g, level, p])
            return 0

        lax.fori_loop(0, blocks // 2, step, 0, unroll=min(4, blocks // 2))

    def last(j, _):
        rows = pl.ds(pl.multiple_of(j * leaf, leaf), leaf)
        grad_ref[0, rows] = dot(in_ref[0, rows], state[j]).astype(BF16)
        return 0

    lax.fori_loop(0, blocks, last, 0, unroll=min(4, blocks))


def body(columns, in_basis, out_basis, transfer, true_ranks, target):
    groups, row_count, rhs = columns.shape
    rank = in_basis.shape[2]
    levels, blocks = transfer.shape[1], transfer.shape[2]
    leaf = row_count // blocks
    local_levels = blocks.bit_length() - 1
    width = rhs // COLUMN_PARTS
    parts = min(BLOCK_PARTS, blocks)
    part = blocks // parts
    size = min(4, part)
    steps = part // size

    def call(kernel, grid, in_specs, out_specs, out_shape, operands, flops, scratch=(), alias=None):
        nbytes = 2 * sum(o.size for o in jax.tree.leaves(out_shape))
        nbytes += flops // 256
        return pl.pallas_call(
            kernel,
            grid_spec=pltpu.PrefetchScalarGridSpec(
                num_scalar_prefetch=1, grid=(grid,), in_specs=in_specs, out_specs=out_specs,
                scratch_shapes=scratch,
            ),
            out_shape=out_shape,
            input_output_aliases=alias or {},
            cost_estimate=pl.CostEstimate(flops=flops, bytes_accessed=nbytes, transcendentals=0),
            compiler_params=pltpu.CompilerParams(vmem_limit_bytes=VMEM_LIMIT),
        )(true_ranks, *operands)

    chunk = jax.ShapeDtypeStruct((groups, part, rank, width), BF16)
    chunk_spec = pl.BlockSpec((groups, size, rank, width), lambda i, r: (0, i, 0, 0))
    group_spec = pl.BlockSpec((1, part, rank, width), lambda g, r: (g, 0, 0, 0))
    any_spec = pl.BlockSpec(memory_space=pl.ANY)
    unit = 2 * groups * part * rank * rank * width

    def level_spec(level, b):
        return pl.BlockSpec(
            (groups, 1, size, 2, rank, rank), lambda i, r: (0, level, b * steps + i, 0, 0, 0)
        )

    def local_spec(count):
        return pl.BlockSpec(
            (1, count, blocks, 2, rank, rank), lambda g, r: (g, 0, 0, 0, 0, 0)
        )

    def basis_spec(b):
        return pl.BlockSpec((groups, size * leaf, rank), lambda i, r: (0, b * steps + i, 0))

    def start(c):
        return call(
            functools.partial(start_kernel, local_levels, leaf),
            groups,
            [
                pl.BlockSpec((1, row_count, rank), lambda g, r: (g, 0, 0)),
                pl.BlockSpec((1, row_count, width), lambda g, r: (g, 0, c)),
                local_spec(local_levels),
            ],
            [group_spec] * parts,
            [chunk] * parts,
            (in_basis, columns, transfer),
            unit * parts * 2 * (local_levels + 1),
            scratch=[pltpu.VMEM((blocks, rank, width), BF16)],
        )

    def forward(level, b, s):
        p = partner_of(s, level - local_levels)
        if level < levels - 1:
            return call(
                functools.partial(level_kernel, level, b * part),
                steps,
                [chunk_spec, chunk_spec, level_spec(level, b)],
                chunk_spec,
                chunk,
                (s, p, transfer),
                unit * 2,
            )
        return call(
            functools.partial(image_kernel, level, b * part, leaf),
            steps,
            [chunk_spec, chunk_spec, level_spec(level, b), basis_spec(b)],
            pl.BlockSpec((size * leaf, width), lambda i, r: (i, 0)),
            jax.ShapeDtypeStruct((part * leaf, width), BF16),
            (s, p, transfer, out_basis),
            unit * 4,
        )

    def at_residual(c, b, summed, residual):
        row_spec = pl.BlockSpec((size * leaf, width), lambda i, r: (b * steps + i, c))
        operands = [summed, target, out_basis, transfer]
        specs = [
            pl.BlockSpec((size * leaf, width), lambda i, r: (i, 0)),
            row_spec,
            basis_spec(b),
            level_spec(levels - 1, b),
        ]
        if residual is not None:
            operands.append(residual)
            specs.append(any_spec)
        return call(
            functools.partial(residual_kernel, levels - 1, b * part, leaf),
            steps,
            specs,
            [row_spec, chunk_spec, chunk_spec],
            [jax.ShapeDtypeStruct((row_count, rhs), BF16), chunk, chunk],
            operands,
            unit * 3,
            alias={5: 0} if residual is not None else None,
        )

    def backward(level, b, back, arriving):
        return call(
            functools.partial(back_kernel, level, b * part),
            steps,
            [chunk_spec, chunk_spec, level_spec(level, b), level_spec(level - 1, b)],
            [chunk_spec, chunk_spec],
            [chunk, chunk],
            (back, arriving, transfer, transfer),
            unit * 2,
        )

    def end(c, backs, arrs, gradient):
        operands = [*backs, *arrs, transfer, in_basis]
        specs = [group_spec] * (2 * parts) + [
            local_spec(local_levels + 1),
            pl.BlockSpec((1, row_count, rank), lambda g, r: (g, 0, 0)),
        ]
        if gradient is not None:
            operands.append(gradient)
            specs.append(any_spec)
        return call(
            functools.partial(end_kernel, local_levels, parts, leaf),
            groups,
            specs,
            pl.BlockSpec((1, row_count, width), lambda g, r: (g, 0, c)),
            jax.ShapeDtypeStruct((groups, row_count, rhs), BF16),
            operands,
            unit * parts * 2 * (local_levels + 1),
            scratch=[pltpu.VMEM((blocks, rank, width), BF16)],
            alias={len(operands): 0} if gradient is not None else None,
        )

    residual = None
    gradient = None
    kept = {}
    previous = None
    for c in range(COLUMN_PARTS):
        states = start(c)
        for b in range(parts):
            s = states[b]
            for level in range(local_levels, levels):
                s = forward(level, b, s)
            if previous is not None:
                s, previous = lax.optimization_barrier((s, previous))
            previous = lax.psum(s, "grp")
            kept[c, b] = previous
    for c in range(COLUMN_PARTS):
        backs, arrs = [], []
        for b in range(parts):
            residual, back, across = at_residual(c, b, kept[c, b], residual)
            for level in reversed(range(local_levels, levels)):
                arriving = partner_of(across, level - local_levels)
                if level > local_levels:
                    back, across = backward(level, b, back, arriving)
            backs.append(back)
            arrs.append(arriving)
        gradient = end(c, backs, arrs, gradient)
    return gradient, residual


def solution(mesh):
    return jax.shard_map(
        body,
        mesh=mesh,
        in_specs=(
            P("grp", "sub", None),
            P("grp", "sub", None),
            P("grp", "sub", None),
            P("grp", None, "sub", None, None, None),
            P("grp", None, "sub"),
            P("sub", None),
        ),
        out_specs=(P("grp", "sub", None), P("sub", None)),
        check_vma=False,
    )
```
